256 devices in a mesh: blk: 32 (over x, y, core), inner: 8 (over z).
Axes of the slice: x: 4, y: 4, z: 8, core: 2. Of those that a mesh axis runs over, the one named last changes fastest.
Arguments:
- latents: bfloat16 [393216, 2048], P(('blk', 'inner')), may hold values from -60 to 60
- test_matrix: bfloat16 [2048, 320], replicated, may hold values from -6 to 6
Outputs:
- basis_rows: float32 [393216, 320], P(('blk', 'inner'))
- projection: float32 [320, 2048], replicated
The draws below stay inside these ranges and needn't reach their ends.
All inputs are finite; a program needn't handle non-finite values.
Results may differ from the reference program's by a relative error of at most 0.00039.
Values sent between devices are 32-bit elements; how exact they have to be, the bound alone decides.
No kernel may reach another device: no remote copies, remote signals or barrier semaphores. Data moves between devices by JAX's collectives and lax.ppermute only.
A program may use at most 64 MiB of HBM per device.

```python
import jax
import jax.numpy as jnp
from jax import lax

W = 2048
K = 320
TOTAL_ROWS = 393216


def draw_latents(key, part):
    key = jax.random.fold_in(key, 11)
    first, second = jax.random.split(key, 2)
    row_index = jnp.arange(TOTAL_ROWS, dtype=jnp.float32)[:, None]
    rising = 1.0 + 2.0 * row_index / TOTAL_ROWS
    row_scale = jnp.exp(jax.random.uniform(second, (TOTAL_ROWS, 1), jnp.float32) * jnp.log(10.0)) / 3.0
    base_values = jnp.clip(jax.random.normal(first, (TOTAL_ROWS, W), jnp.float32), -5.0, 5.0)
    return (base_values * rising * row_scale).astype(jnp.bfloat16)


def bell_draw(own_key, extent, width, limit, kind=jnp.bfloat16):
    array = width * jax.random.normal(own_key, extent, jnp.float32)
    return jnp.clip(array, min=-limit, max=limit).astype(kind)


def setup_inputs(seed: int = 0) -> dict:
    splits = jax.random.split(jax.random.key(seed), 3)
    latents = draw_latents(jax.random.fold_in(splits[2], 71), 0)
    test_matrix = bell_draw(splits[1], (W, K), 1.0, 6.0)
    return {"latents": latents, "test_matrix": test_matrix}


def reference(latents, test_matrix):
    sketch = jnp.dot(latents.astype(jnp.float32), test_matrix.astype(jnp.float32), preferred_element_type=jnp.float32)
    gram = jnp.dot(sketch.T.astype(jnp.float32), sketch.astype(jnp.float32), preferred_element_type=jnp.float32, precision=lax.Precision.HIGHEST) / TOTAL_ROWS
    lower_factor = jnp.linalg.cholesky(gram)
    basis_rows = jax.scipy.linalg.solve_triangular(lower_factor, sketch.T, lower=True).T
    sketch_low = sketch.astype(jnp.bfloat16)
    cross = jnp.dot(sketch_low.T.astype(jnp.float32), latents.astype(jnp.float32), preferred_element_type=jnp.float32)
    solved = jax.scipy.linalg.solve_triangular(lower_factor, cross, lower=True)
    projection = solved * (jnp.sqrt(jnp.float32(W)) / TOTAL_ROWS)
    return (basis_rows, projection)
```

```python
import functools

import jax
import jax.numpy as jnp
from jax import lax
from jax.experimental import pallas as pl
from jax.experimental.pallas import tpu as pltpu
from jax.sharding import PartitionSpec as P

HIGHEST = lax.Precision.HIGHEST
LANES = 128
STEP = 8


def dot(a, b):
    return jnp.dot(a, b, precision=HIGHEST, preferred_element_type=jnp.float32)


def dot_t(a, b):
    return lax.dot_general(
        a, b, (((0,), (0,)), ((), ())), precision=HIGHEST, preferred_element_type=jnp.float32
    )


def reciprocal(d):
    r = pl.reciprocal(d, approx=True)
    r = r * (2.0 - d * r)
    return r * (2.0 - d * r)


def factor_inverse(w, n):
    count = n // 8
    tiles = [w[8 * t : 8 * t + 8, :] for t in range(count)]
    lane = lax.broadcasted_iota(jnp.int32, (8, LANES), 1)
    sub = lax.broadcasted_iota(jnp.int32, (8, LANES), 0)
    pivots = []

    def over_lanes(x, j):
        return jnp.broadcast_to(x[:, j : j + 1], (8, LANES))

    def over_rows(x, i):
        return jnp.broadcast_to(x[i : i + 1, :], (8, LANES))

    for first in range(count):
        j = 8 * first
        cols = [{t: over_lanes(tiles[t], j + k) for t in range(first, count)} for k in range(STEP)]
        group = (lane >= j) & (lane < j + STEP)
        coefs = []
        pivot = jnp.zeros((8, LANES), jnp.float32)
        for k in range(STEP):
            d = over_rows(cols[k][first], k)
            pivot = jnp.where(sub == k, d, pivot)
            inverse = reciprocal(d)
            coef = {t: cols[k][t] * inverse for t in range(first, count)}
            coef[first] = jnp.where(sub > k, coef[first], 0.0)
            coefs.append(coef)
            for m in range(k + 1, STEP):
                value = over_rows(cols[k][first], m)
                for t in range(first, count):
                    cols[m][t] = cols[m][t] - coef[t] * value
        pivots.append(pivot)
        current = jnp.where(group, 0.0, tiles[first])
        rows = []
        for k in range(STEP):
            row = jnp.where(lane == j + k, 1.0, over_rows(current, k))
            rows.append(row)
            current = current - coefs[k][first] * row
        tiles[first] = jnp.where(lane == j + sub, 1.0, current)
        for t in range(first + 1, count):
            x = jnp.where(group, 0.0, tiles[t])
            for k in range(STEP):
                x = x - coefs[k][t] * rows[k]
            tiles[t] = x
    out = []
    for t in range(count):
        out.append(jnp.where(lane <= sub + 8 * t, tiles[t] * lax.rsqrt(pivots[t]), 0.0))
    return jnp.concatenate(out, axis=0)


def chol_kernel(g_ref, m_ref):
    m0 = factor_inverse(g_ref[0:128, 0:128], 128)
    a01 = dot(m0, g_ref[0:128, 128:384])
    m_ref[0:128, 0:128] = m0
    m_ref[0:128, 128:384] = jnp.zeros((128, 256), jnp.float32)
    s11 = g_ref[128:256, 128:256] - dot_t(a01[:, 0:128], a01[:, 0:128])
    m1 = factor_inverse(s11, 128)
    s12 = g_ref[128:256, 256:384] - dot_t(a01[:, 0:128], a01[:, 128:256])
    s22 = g_ref[256:384, 256:384] - dot_t(a01[:, 128:256], a01[:, 128:256])
    b0 = -dot_t(a01, m0)
    a12 = dot(m1, s12)
    s22 = s22 - dot_t(a12, a12)
    m2 = factor_inverse(s22[0:64], 64)
    b10 = dot(m1, b0[0:128])
    m_ref[128:256, 0:128] = b10
    m_ref[128:256, 128:256] = m1
    m_ref[128:256, 256:384] = jnp.zeros((128, 128), jnp.float32)
    b20 = b0[128:192] - dot_t(a12, b10)[0:64]
    b21 = -dot_t(a12, m1)[0:64]
    m_ref[256:320, 0:128] = dot(m2[:, 0:64], b20)
    m_ref[256:320, 128:256] = dot(m2[:, 0:64], b21)
    m_ref[256:320, 256:384] = m2


def chol_inverse(gram):
    return pl.pallas_call(
        chol_kernel,
        out_shape=jax.ShapeDtypeStruct((320, 384), jnp.float32),
        in_specs=[pl.BlockSpec(memory_space=pltpu.VMEM)],
        out_specs=pl.BlockSpec(memory_space=pltpu.VMEM),
        compiler_params=pltpu.CompilerParams(vmem_limit_bytes=32 * 2**20),
        cost_estimate=pl.CostEstimate(flops=10**9, bytes_accessed=10**6, transcendentals=0),
        name="chol_inverse",
    )(gram)


def all_reduced(parts, mine):
    rows = parts.shape[2]
    swap = [(i, i ^ 1) for i in range(lax.axis_size("blk"))]
    chips = lax.axis_size("blk") // 2
    groups = [[2 * i + core for i in range(chips)] for core in range(2)]
    depth = lax.axis_size("inner")

    def exchanged(value):
        return lax.all_to_all(value, "blk", 0, 0, axis_index_groups=groups)

    keep = lax.dynamic_index_in_dim(parts, mine, 0, keepdims=False)
    give = lax.dynamic_index_in_dim(parts, 1 - mine, 0, keepdims=False)
    half = keep + lax.ppermute(give, "blk", swap)
    chunk = exchanged(half).sum(0)
    shares = chunk.reshape(depth, rows // depth, LANES)
    share = lax.all_to_all(shares, "inner", 0, 0).sum(0)
    copies = jnp.broadcast_to(share[None], shares.shape)
    chunk = lax.all_to_all(copies, "inner", 0, 0).reshape(rows, LANES)
    half = exchanged(jnp.broadcast_to(chunk[None], half.shape))
    other = lax.ppermute(half, "blk", swap)
    first = jnp.where(mine == 0, half, other)
    second = jnp.where(mine == 0, other, half)
    return jnp.concatenate([first, second], axis=0)


def shards(latents, test_matrix):
    width = latents.shape[1]
    sketch_width = test_matrix.shape[1]
    row_total = latents.shape[0] * lax.axis_size("blk") * lax.axis_size("inner")
    sketch = jnp.dot(latents, test_matrix, preferred_element_type=jnp.float32)
    gram_local = dot_t(sketch, sketch) / row_total
    cross_local = lax.dot_general(
        sketch.astype(jnp.bfloat16),
        latents,
        (((0,), (0,)), ((), ())),
        preferred_element_type=jnp.float32,
    )

    def by_tiles(value, tiles):
        value = jnp.pad(value, ((0, 0), (0, tiles * LANES - value.shape[1])))
        return value.reshape(sketch_width, tiles, LANES).swapaxes(0, 1).reshape(-1, 10, LANES)

    cross_rows = by_tiles(cross_local, width // LANES).reshape(32, 160, LANES)
    gram_rows = by_tiles(gram_local, 3).reshape(32, 30, LANES)
    parts = jnp.concatenate(
        [cross_rows, gram_rows, jnp.zeros((32, 2, LANES), jnp.float32)], axis=1
    )
    mine = lax.axis_index("blk") % 2
    total = all_reduced(parts.reshape(2, 16, 192, LANES), mine)

    def from_tiles(value, tiles):
        value = value.reshape(tiles, sketch_width, LANES).swapaxes(0, 1)
        return value.reshape(sketch_width, tiles * LANES)

    gram = jnp.pad(from_tiles(total[:, 160:190], 3), ((0, 64), (0, 0)))
    cross = from_tiles(total[:, :160], width // LANES)
    inverse = chol_inverse(gram)[:, :sketch_width]
    basis_rows = lax.dot_general(
        sketch,
        inverse,
        (((1,), (1,)), ((), ())),
        precision=HIGHEST,
        preferred_element_type=jnp.float32,
    )
    projection = dot(inverse, cross) * (jnp.sqrt(jnp.float32(width)) / row_total)
    return (basis_rows, projection)


def solution(mesh):
    placed = (P(("blk", "inner"), None), P())
    return jax.shard_map(
        shards,
        mesh=mesh,
        in_specs=placed,
        out_specs=(P(("blk", "inner"), None), P()),
        check_vma=False,
    )
```

```python
import functools

import jax
import jax.numpy as jnp
from jax import lax
from jax.experimental import pallas as pl
from jax.experimental.pallas import tpu as pltpu
from jax.sharding import PartitionSpec as P

HIGHEST = lax.Precision.HIGHEST
LANES = 128
STEP = 8


def dot(a, b):
    return jnp.dot(a, b, precision=HIGHEST, preferred_element_type=jnp.float32)


def dot_t(a, b):
    return lax.dot_general(
        a, b, (((0,), (0,)), ((), ())), precision=HIGHEST, preferred_element_type=jnp.float32
    )


def factor_inverse(w, n, scratch):
    count = n // 8
    tiles = [w[8 * t : 8 * t + 8, :] for t in range(count)]
    lane = lax.broadcasted_iota(jnp.int32, (8, LANES), 1)
    sub = lax.broadcasted_iota(jnp.int32, (8, LANES), 0)
    pivots = []

    def over_lanes(x, j):
        return jnp.broadcast_to(x[:, j : j + 1], (8, LANES))

    for first in range(count):
        j = STEP * first
        base = 9 * STEP * first
        group = (lane >= j) & (lane < j + STEP)

        def row(i, base=base):
            return jnp.broadcast_to(scratch[base + i : base + i + 1, :], (8, LANES))

        for k in range(STEP):
            scratch[base + 8 * k : base + 8 * k + 8, :] = over_lanes(tiles[first], j + k)
        scratch[base + 64 : base + 72, :] = jnp.where(group, 0.0, tiles[first])
        square = [[row(8 * k + m) for k in range(m + 1)] for m in range(STEP)]
        rows = [row(64 + m) for m in range(STEP)]
        lower = [[None] * STEP for _ in range(STEP)]
        inverse = []
        pivot = square[0][0]
        for k in range(STEP):
            if k:
                pivot = jnp.where(sub == k, square[k][k], pivot)
            inverse.append(1.0 / square[k][k])
            for m in range(k + 1, STEP):
                lower[m][k] = square[m][k] * inverse[k]
            for m in range(k + 1, STEP):
                for i in range(m, STEP):
                    square[i][m] = square[i][m] - square[i][k] * lower[m][k]
            rows[k] = jnp.where(lane == j + k, 1.0, rows[k])
            for m in range(k + 1, STEP):
                rows[m] = rows[m] - lower[m][k] * rows[k]
        pivots.append(pivot)
        done = rows[0]
        for k in range(1, STEP):
            done = jnp.where(sub == k, rows[k], done)
        tiles[first] = done
        scaled = [rows[k] * inverse[k] for k in range(STEP)]
        for t in range(first + 1, count):
            cols = [over_lanes(tiles[t], j + k) for k in range(STEP)]
            x = jnp.where(group, 0.0, tiles[t])
            for k in range(STEP):
                x = x - cols[k] * scaled[k]
                for m in range(k + 1, STEP):
                    cols[m] = cols[m] - cols[k] * lower[m][k]
            tiles[t] = x
    out = []
    for t in range(count):
        out.append(jnp.where(lane <= sub + 8 * t, tiles[t] * lax.rsqrt(pivots[t]), 0.0))
    return jnp.concatenate(out, axis=0)


def bf16_parts(x):
    high = x.astype(jnp.bfloat16)
    return high, (x - high.astype(jnp.float32)).astype(jnp.bfloat16)


def mxu(a, b, dims=((1,), (0,))):
    return lax.dot_general(a, b, (dims, ((), ())), preferred_element_type=jnp.float32)


ROWS_OF = ((1,), (1,))
VMEM = pl.BlockSpec(memory_space=pltpu.VMEM)
SMEM = pl.BlockSpec(memory_space=pltpu.SMEM)
HBM = pl.BlockSpec(memory_space=pltpu.HBM)
CHIPS = 16
DEPTH = 8
BLOCKS = 6


def shape(*dims, dtype=jnp.float32):
    return jax.ShapeDtypeStruct(dims, dtype)


def call(kernel, name, out_shape, in_specs, out_specs, scratch=(), flops=10**6, moved=10**6, mib=24):
    return pl.pallas_call(
        kernel,
        out_shape=out_shape,
        in_specs=in_specs,
        out_specs=out_specs,
        scratch_shapes=list(scratch),
        compiler_params=pltpu.CompilerParams(vmem_limit_bytes=mib * 2**20),
        cost_estimate=pl.CostEstimate(flops=flops, bytes_accessed=moved, transcendentals=0),
        name=name,
    )


def front_kernel(
    row_total, core_ref, lat_hbm, om_hbm, high_ref, mid_ref, keep_ref, give_ref, lat, om_ref, low, sems
):
    rows, width = lat.shape
    tall = om_ref.shape[0]
    block = rows // BLOCKS
    core = core_ref[0]

    def load(i):
        part = pl.ds(pl.multiple_of(i * block, block), block)
        return pltpu.make_async_copy(lat_hbm.at[part], lat.at[part], sems.at[i])

    test = pltpu.make_async_copy(om_hbm, om_ref, sems.at[BLOCKS])
    test.start()
    for i in range(BLOCKS):
        load(i).start()
    test.wait()

    @pl.loop(0, BLOCKS)
    def _(i):
        load(i).wait()
        part = pl.ds(pl.multiple_of(i * block, block), block)
        s = mxu(om_ref[...], lat[part, :], ROWS_OF)
        high, mid = bf16_parts(s)
        high_ref[:, part] = high
        mid_ref[:, part] = mid
        low[:, part] = (s - high.astype(jnp.float32) - mid.astype(jnp.float32)).astype(jnp.bfloat16)

    for ref, which in ((give_ref, 1 - core), (keep_ref, core)):

        @pl.loop(0, width // 512)
        def _(c, ref=ref, which=which):
            at = pl.multiple_of(which * (width // 2) + c * 256, 256)
            out = mxu(high_ref[...], lat[:, pl.ds(at, 256)])
            for k in range(4):
                piece = out[(k % 2) * (tall // 2) : (k % 2 + 1) * (tall // 2)]
                piece = piece[:, (k // 2) * LANES : (k // 2 + 1) * LANES]
                ref[4 * c + k, 0 : tall // 2, :] = piece

    high = high_ref[...]
    mid = mid_ref[...]
    cross_mid = mxu(high, mid, ROWS_OF) + mxu(high, low[...], ROWS_OF)
    gram = mxu(high, high, ROWS_OF) + (cross_mid + cross_mid.T + mxu(mid, mid, ROWS_OF))
    gram = gram * (1.0 / row_total)
    corner = jnp.concatenate([gram[256:320, 256:320], gram[64:128, 64:128]], axis=1)
    zero = jnp.concatenate([gram[0:64, 0:128], corner, gram[0:128, 128:256]], axis=0)
    last = jnp.concatenate([gram[0:128, 256:320], gram[128:256, 256:320]], axis=1)
    one = jnp.concatenate([last, gram[128:256, 128:256]], axis=0)
    own = jnp.where(core == 0, zero, one).reshape(CHIPS, 16, LANES)
    far = jnp.where(core == 0, one, zero).reshape(CHIPS, 16, LANES)
    keep_ref[:, tall // 2 :, :] = own
    give_ref[:, tall // 2 :, :] = far


def front(core, latents, test_t, row_total):
    rows, width = latents.shape
    tall = test_t.shape[0]
    bf16 = jnp.bfloat16
    return call(
        functools.partial(front_kernel, row_total),
        "front",
        [
            shape(tall, rows, dtype=bf16),
            shape(tall, rows, dtype=bf16),
            shape(CHIPS, tall // 2 + 16, LANES),
            shape(CHIPS, tall // 2 + 16, LANES),
        ],
        [SMEM, HBM, HBM],
        [VMEM] * 4,
        [
            pltpu.VMEM((rows, width), bf16),
            pltpu.VMEM((tall, width), bf16),
            pltpu.VMEM((tall, rows), bf16),
            pltpu.SemaphoreType.DMA((BLOCKS + 1,)),
        ],
        flops=6 * 10**9,
        moved=10**7,
        mib=46,
    )(core, latents, test_t)


def sum_copies_kernel(x_ref, out_ref):
    total = x_ref[0]
    for i in range(1, x_ref.shape[0]):
        total = total + x_ref[i]
    for i in range(out_ref.shape[0]):
        out_ref[i] = total


def sum_copies(x, count):
    return call(sum_copies_kernel, "sum_copies", shape(count, *x.shape[1:]), [VMEM], VMEM)(x)


def factor(zero, one, m_ref, scratch):
    left = jnp.concatenate([zero[0:64, 64:128].T, zero[64:128, 64:128]], axis=1)
    g00 = jnp.concatenate([zero[0:64], left], axis=0)
    blank = jnp.zeros((128, 64), jnp.float32)
    g01 = jnp.concatenate([zero[128:256], one[0:128, 0:64], blank], axis=1)
    g12 = jnp.concatenate([one[0:128, 64:128], blank], axis=1)
    g22 = jnp.concatenate([zero[64:128, 0:64], blank[0:64]], axis=1)
    m0 = factor_inverse(g00, 128, scratch)
    a01 = dot(m0, g01)
    m_ref[0:128, 0:128] = m0
    m_ref[0:128, 128:384] = jnp.zeros((128, 256), jnp.float32)
    m1 = factor_inverse(one[128:256] - dot_t(a01[:, 0:128], a01[:, 0:128]), 128, scratch)
    s12 = g12 - dot_t(a01[:, 0:128], a01[:, 128:256])
    s22 = g22 - dot_t(a01[:, 128:256], a01[:, 128:256])[0:64]
    b0 = -dot_t(a01, m0)
    a12 = dot(m1, s12)
    s22 = s22 - dot_t(a12, a12)[0:64]
    m2 = factor_inverse(s22, 64, scratch)
    b10 = dot(m1, b0[0:128])
    m_ref[128:256, 0:128] = b10
    m_ref[128:256, 128:256] = m1
    m_ref[128:256, 256:384] = jnp.zeros((128, 128), jnp.float32)
    b20 = b0[128:192] - dot_t(a12, b10)[0:64]
    b21 = -dot_t(a12, m1)[0:64]
    m_ref[256:320, 0:128] = dot(m2[:, 0:64], b20)
    m_ref[256:320, 128:256] = dot(m2[:, 0:64], b21)
    m_ref[256:320, 256:384] = m2


def lower_product(m, high, low):
    out = []
    for rows, depth in (((0, 256), 256), ((256, 320), 320)):
        m_high, m_low = (part[rows[0] : rows[1], 0:depth] for part in m)
        x_high, x_low = high[0:depth], low[0:depth]
        out.append(mxu(m_high, x_high) + (mxu(m_high, x_low) + mxu(m_low, x_high)))
    return out


def factor_kernel(core_ref, half_ref, far_ref, m_ref, scratch):
    core = core_ref[0]
    own = half_ref[:, half_ref.shape[1] - 16 :, :].reshape(256, LANES)
    far = far_ref[...].reshape(256, LANES)
    factor(jnp.where(core == 0, own, far), jnp.where(core == 0, far, own), m_ref, scratch)


def finish_kernel(
    scale, core_ref, m_ref, half_ref, other_ref, high_hbm, mid_hbm, basis_hbm, proj_hbm,
    high, mid, basis, proj, in_sems, basis_sems, proj_sems,
):
    core = core_ref[0]
    tall, width = proj.shape
    rows = basis.shape[1]
    high_copy = pltpu.make_async_copy(high_hbm, high, in_sems.at[0])
    mid_copy = pltpu.make_async_copy(mid_hbm, mid, in_sems.at[1])
    high_copy.start()
    mid_copy.start()
    inverse = bf16_parts(m_ref[:, 0:tall])
    scaled = bf16_parts(m_ref[:, 0:tall] * scale)
    steps = width // 512

    def proj_copy(which, c):
        at = pl.multiple_of(which * (width // 2) + c * 256, 256)
        part = (slice(None), pl.ds(at, 256))
        number = which * steps + c
        return at, pltpu.make_async_copy(proj.at[part], proj_hbm.at[part], proj_sems.at[number])

    for ref, which in ((half_ref, core), (other_ref, 1 - core)):

        @pl.loop(0, steps)
        def _(c, ref=ref, which=which):
            tiles = ref[pl.ds(4 * c, 4), 0 : tall // 2, :].reshape(2, tall, LANES)
            cross = jnp.concatenate([tiles[0], tiles[1]], axis=1)
            at, move = proj_copy(which, c)
            upper, lower = lower_product(scaled, *bf16_parts(cross))
            proj[0:256, pl.ds(at, 256)] = upper
            proj[256:320, pl.ds(at, 256)] = lower
            move.start()

    high_copy.wait()
    mid_copy.wait()
    block = rows // BLOCKS

    def basis_copy(i):
        part = (slice(None), pl.ds(pl.multiple_of(i * block, block), block))
        return pltpu.make_async_copy(basis.at[part], basis_hbm.at[part], basis_sems.at[i])

    @pl.loop(0, BLOCKS)
    def _(i):
        part = pl.ds(pl.multiple_of(i * block, block), block)
        upper, lower = lower_product(inverse, high[:, part], mid[:, part])
        basis[0:256, part] = upper
        basis[256:320, part] = lower
        basis_copy(i).start()

    for which in range(2):

        @pl.loop(0, steps)
        def _(c, which=which):
            proj_copy(which, c)[1].wait()

    @pl.loop(0, BLOCKS)
    def _(i):
        basis_copy(i).wait()


def shards(latents, test_matrix):
    rows, width = latents.shape
    tall = test_matrix.shape[1]
    row_total = rows * lax.axis_size("blk") * lax.axis_size("inner")
    core = (lax.axis_index("blk") % 2).astype(jnp.int32).reshape(1)
    swap = [(i, i ^ 1) for i in range(2 * CHIPS)]
    groups = [[2 * i + side for i in range(CHIPS)] for side in range(2)]

    def over_chips(value):
        return lax.all_to_all(value, "blk", 0, 0, axis_index_groups=groups)

    high, mid, keep, give = front(core, latents, test_matrix.T, row_total)
    chunks = over_chips(keep + lax.ppermute(give, "blk", swap))
    chunk = lax.all_to_all(sum_copies(chunks, DEPTH), "inner", 0, 0)
    half = over_chips(sum_copies(chunk, CHIPS))
    gram_far = lax.ppermute(half[:, tall // 2 :], "blk", swap)
    half, gram_far = lax.optimization_barrier((half, gram_far))
    other = lax.ppermute(half, "blk", swap)
    inverse = call(
        factor_kernel,
        "factor",
        shape(tall, 384),
        [SMEM, VMEM, VMEM],
        VMEM,
        [pltpu.VMEM((9 * LANES, LANES), jnp.float32)],
        flops=12 * 10**9,
    )(core, half, gram_far)
    bf16 = jnp.bfloat16
    basis_t, projection = call(
        functools.partial(finish_kernel, float(width) ** 0.5 / row_total),
        "finish",
        [shape(tall, rows), shape(tall, width)],
        [SMEM, VMEM, VMEM, VMEM, HBM, HBM],
        [HBM, HBM],
        [
            pltpu.VMEM((tall, rows), bf16),
            pltpu.VMEM((tall, rows), bf16),
            pltpu.VMEM((tall, rows), jnp.float32),
            pltpu.VMEM((tall, width), jnp.float32),
            pltpu.SemaphoreType.DMA((2,)),
            pltpu.SemaphoreType.DMA((BLOCKS,)),
            pltpu.SemaphoreType.DMA((width // 256,)),
        ],
        flops=3 * 10**9,
        moved=10**7,
    )(core, inverse, half, other, high, mid)
    return (basis_t.T, projection)


def solution(mesh):
    placed = (P(("blk", "inner"), None), P())
    return jax.shard_map(
        shards,
        mesh=mesh,
        in_specs=placed,
        out_specs=(P(("blk", "inner"), None), P()),
        check_vma=False,
    )
```

```python
import functools

import jax
import jax.numpy as jnp
from jax import lax
from jax.experimental import pallas as pl
from jax.experimental.pallas import tpu as pltpu
from jax.sharding import PartitionSpec as P

HIGHEST = lax.Precision.HIGHEST
LANES = 128
STEP = 8


def dot(a, b):
    return jnp.dot(a, b, precision=HIGHEST, preferred_element_type=jnp.float32)


def dot_t(a, b):
    return lax.dot_general(
        a, b, (((0,), (0,)), ((), ())), precision=HIGHEST, preferred_element_type=jnp.float32
    )


def factor_inverse(w, n, scratch):
    count = n // 8
    tiles = [w[8 * t : 8 * t + 8, :] for t in range(count)]
    lane = lax.broadcasted_iota(jnp.int32, (8, LANES), 1)
    sub = lax.broadcasted_iota(jnp.int32, (8, LANES), 0)
    pivots = []

    def over_lanes(x, j):
        return jnp.broadcast_to(x[:, j : j + 1], (8, LANES))

    for first in range(count):
        j = STEP * first
        base = 9 * STEP * first
        group = (lane >= j) & (lane < j + STEP)

        def row(i, base=base):
            return jnp.broadcast_to(scratch[base + i : base + i + 1, :], (8, LANES))

        for k in range(STEP):
            scratch[base + 8 * k : base + 8 * k + 8, :] = over_lanes(tiles[first], j + k)
        scratch[base + 64 : base + 72, :] = jnp.where(group, 0.0, tiles[first])
        square = [[row(8 * k + m) for k in range(m + 1)] for m in range(STEP)]
        rows = [row(64 + m) for m in range(STEP)]
        lower = [[None] * STEP for _ in range(STEP)]
        inverse = []
        pivot = square[0][0]
        for k in range(STEP):
            if k:
                pivot = jnp.where(sub == k, square[k][k], pivot)
            inverse.append(1.0 / square[k][k])
            for m in range(k + 1, STEP):
                lower[m][k] = square[m][k] * inverse[k]
            for m in range(k + 1, STEP):
                for i in range(m, STEP):
                    square[i][m] = square[i][m] - square[i][k] * lower[m][k]
            rows[k] = jnp.where(lane == j + k, 1.0, rows[k])
            for m in range(k + 1, STEP):
                rows[m] = rows[m] - lower[m][k] * rows[k]
        pivots.append(pivot)
        done = rows[0]
        for k in range(1, STEP):
            done = jnp.where(sub == k, rows[k], done)
        tiles[first] = done
        scaled = [rows[k] * inverse[k] for k in range(STEP)]
        for t in range(first + 1, count):
            cols = [over_lanes(tiles[t], j + k) for k in range(STEP)]
            x = jnp.where(group, 0.0, tiles[t])
            for k in range(STEP):
                x = x - cols[k] * scaled[k]
                for m in range(k + 1, STEP):
                    cols[m] = cols[m] - cols[k] * lower[m][k]
            tiles[t] = x
    out = []
    for t in range(count):
        out.append(jnp.where(lane <= sub + 8 * t, tiles[t] * lax.rsqrt(pivots[t]), 0.0))
    return jnp.concatenate(out, axis=0)


def bf16_parts(x):
    high = x.astype(jnp.bfloat16)
    return high, (x - high.astype(jnp.float32)).astype(jnp.bfloat16)


def mxu(a, b, dims=((1,), (0,))):
    return lax.dot_general(a, b, (dims, ((), ())), preferred_element_type=jnp.float32)


ROWS_OF = ((1,), (1,))
VMEM = pl.BlockSpec(memory_space=pltpu.VMEM)
SMEM = pl.BlockSpec(memory_space=pltpu.SMEM)
HBM = pl.BlockSpec(memory_space=pltpu.HBM)
CHIPS = 16
DEPTH = 8
BLOCKS = 3
LOADS = 3


def shape(*dims, dtype=jnp.float32):
    return jax.ShapeDtypeStruct(dims, dtype)


def call(kernel, name, out_shape, in_specs, out_specs, scratch=(), flops=10**6, moved=10**6, mib=24):
    return pl.pallas_call(
        kernel,
        out_shape=out_shape,
        in_specs=in_specs,
        out_specs=out_specs,
        scratch_shapes=list(scratch),
        compiler_params=pltpu.CompilerParams(vmem_limit_bytes=mib * 2**20),
        cost_estimate=pl.CostEstimate(flops=flops, bytes_accessed=moved, transcendentals=0),
        name=name,
    )


def front_kernel(
    row_total, core_ref, lat_hbm, om_hbm, high_ref, mid_ref, keep_ref, give_ref, lat, om, parts, sems
):
    rows, width = lat.shape
    tall = om.shape[0]
    block = rows // LOADS
    core = core_ref[0]

    def load(i):
        part = pl.ds(i * block, block)
        return pltpu.make_async_copy(lat_hbm.at[part], lat.at[part], sems.at[i])

    test = pltpu.make_async_copy(om_hbm, om, sems.at[LOADS])
    test.start()
    for i in range(LOADS):
        load(i).start()
    test.wait()
    for i in range(LOADS):
        load(i).wait()
        part = pl.ds(i * block, block)
        s = mxu(om[...], lat[part, :], ROWS_OF)
        high, mid = bf16_parts(s)
        low = (s - high.astype(jnp.float32) - mid.astype(jnp.float32)).astype(jnp.bfloat16)
        high_ref[:, part] = high
        mid_ref[:, part] = mid
        parts[0:tall, part] = high
        parts[tall : 2 * tall, part] = mid
        parts[2 * tall :, part] = low

    for ref, which in ((give_ref, 1 - core), (keep_ref, core)):
        at = pl.multiple_of(which * (width // 2), width // 2)
        out = mxu(parts[0:tall, :], lat[:, pl.ds(at, width // 2)])
        for j in range(CHIPS):
            rows_from = (j % 2) * (tall // 2)
            lanes_from = (j // 2) * LANES
            ref[j, 0 : tall // 2, :] = out[
                rows_from : rows_from + tall // 2, lanes_from : lanes_from + LANES
            ]

    by_high = mxu(parts[0:tall, :], parts[...], ROWS_OF)
    mixed = by_high[:, tall : 2 * tall] + by_high[:, 2 * tall :]
    mid = parts[tall : 2 * tall, :]
    gram = by_high[:, 0:tall] + (mixed + mixed.T + mxu(mid, mid, ROWS_OF))
    gram = gram * (1.0 / row_total)
    corner = jnp.concatenate([gram[256:320, 256:320], gram[64:128, 64:128]], axis=1)
    zero = jnp.concatenate([gram[0:64, 0:128], corner, gram[0:128, 128:256]], axis=0)
    last = jnp.concatenate([gram[0:128, 256:320], gram[128:256, 256:320]], axis=1)
    one = jnp.concatenate([last, gram[128:256, 128:256]], axis=0)
    own = jnp.where(core == 0, zero, one).reshape(CHIPS, 16, LANES)
    far = jnp.where(core == 0, one, zero).reshape(CHIPS, 16, LANES)
    keep_ref[:, tall // 2 :, :] = own
    give_ref[:, tall // 2 :, :] = far


def front(core, latents, test_t, row_total):
    rows, width = latents.shape
    tall = test_t.shape[0]
    bf16 = jnp.bfloat16
    return call(
        functools.partial(front_kernel, row_total),
        "front",
        [
            shape(tall, rows, dtype=bf16),
            shape(tall, rows, dtype=bf16),
            shape(CHIPS, tall // 2 + 16, LANES),
            shape(CHIPS, tall // 2 + 16, LANES),
        ],
        [SMEM, HBM, HBM],
        [VMEM] * 4,
        [
            pltpu.VMEM((rows, width), bf16),
            pltpu.VMEM((tall, width), bf16),
            pltpu.VMEM((3 * tall, rows), bf16),
            pltpu.SemaphoreType.DMA((LOADS + 1,)),
        ],
        flops=6 * 10**9,
        moved=10**7,
        mib=46,
    )(core, latents, test_t)


def sum_copies_kernel(x_ref, out_ref):
    total = x_ref[0]
    for i in range(1, x_ref.shape[0]):
        total = total + x_ref[i]
    for i in range(out_ref.shape[0]):
        out_ref[i] = total


def sum_copies(x, count):
    return call(sum_copies_kernel, "sum_copies", shape(count, *x.shape[1:]), [VMEM], VMEM)(x)


def factor(zero, one, m_ref, scratch):
    left = jnp.concatenate([zero[0:64, 64:128].T, zero[64:128, 64:128]], axis=1)
    g00 = jnp.concatenate([zero[0:64], left], axis=0)
    blank = jnp.zeros((128, 64), jnp.float32)
    g01 = jnp.concatenate([zero[128:256], one[0:128, 0:64], blank], axis=1)
    g12 = jnp.concatenate([one[0:128, 64:128], blank], axis=1)
    g22 = jnp.concatenate([zero[64:128, 0:64], blank[0:64]], axis=1)
    m0 = factor_inverse(g00, 128, scratch)
    a01 = dot(m0, g01)
    m_ref[0:128, 0:128] = m0
    m_ref[0:128, 128:384] = jnp.zeros((128, 256), jnp.float32)
    m1 = factor_inverse(one[128:256] - dot_t(a01[:, 0:128], a01[:, 0:128]), 128, scratch)
    s12 = g12 - dot_t(a01[:, 0:128], a01[:, 128:256])
    s22 = g22 - dot_t(a01[:, 128:256], a01[:, 128:256])[0:64]
    b0 = -dot_t(a01, m0)
    a12 = dot(m1, s12)
    s22 = s22 - dot_t(a12, a12)[0:64]
    m2 = factor_inverse(s22, 64, scratch)
    b10 = dot(m1, b0[0:128])
    m_ref[128:256, 0:128] = b10
    m_ref[128:256, 128:256] = m1
    m_ref[128:256, 256:384] = jnp.zeros((128, 128), jnp.float32)
    b20 = b0[128:192] - dot_t(a12, b10)[0:64]
    b21 = -dot_t(a12, m1)[0:64]
    m_ref[256:320, 0:128] = dot(m2[:, 0:64], b20)
    m_ref[256:320, 128:256] = dot(m2[:, 0:64], b21)
    m_ref[256:320, 256:384] = m2


def lower_product(m, high, low):
    out = []
    for rows, depth in (((0, 256), 256), ((256, 320), 320)):
        m_high, m_low = (part[rows[0] : rows[1], 0:depth] for part in m)
        x_high, x_low = high[0:depth], low[0:depth]
        out.append(mxu(m_high, x_high) + (mxu(m_high, x_low) + mxu(m_low, x_high)))
    return out


def factor_kernel(core_ref, half_ref, far_ref, m_ref, scratch):
    core = core_ref[0]
    own = half_ref[:, half_ref.shape[1] - 16 :, :].reshape(256, LANES)
    far = far_ref[...].reshape(256, LANES)
    factor(jnp.where(core == 0, own, far), jnp.where(core == 0, far, own), m_ref, scratch)


def finish_kernel(
    scale, core_ref, m_ref, half_ref, other_ref, high_hbm, mid_hbm, basis_hbm, proj_hbm,
    high, mid, basis, proj, in_sems, basis_sems, proj_sems,
):
    core = core_ref[0]
    tall, width = proj.shape
    rows = basis.shape[1]
    high_copy = pltpu.make_async_copy(high_hbm, high, in_sems.at[0])
    mid_copy = pltpu.make_async_copy(mid_hbm, mid, in_sems.at[1])
    high_copy.start()
    mid_copy.start()
    inverse = bf16_parts(m_ref[:, 0:tall])
    step = width // 4
    copies = []
    for c in range(4):
        ref, which = (half_ref, core) if c < 2 else (other_ref, 1 - core)
        tiles = ref[8 * (c % 2) : 8 * (c % 2) + 8, 0 : tall // 2, :].reshape(4, tall, LANES)
        cross = jnp.concatenate([tiles[i] for i in range(4)], axis=1)
        upper, lower = lower_product(inverse, *bf16_parts(cross))
        proj[0:256, c * step : (c + 1) * step] = upper * scale
        proj[256:320, c * step : (c + 1) * step] = lower * scale
        there = pl.ds(pl.multiple_of(which * (2 * step) + (c % 2) * step, step), step)
        copies.append(
            pltpu.make_async_copy(
                proj.at[:, pl.ds(c * step, step)], proj_hbm.at[:, there], proj_sems.at[c]
            )
        )
        copies[-1].start()
    high_copy.wait()
    mid_copy.wait()
    block = rows // BLOCKS
    for i in range(BLOCKS):
        part = pl.ds(i * block, block)
        upper, lower = lower_product(inverse, high[:, part], mid[:, part])
        basis[0:256, part] = upper
        basis[256:320, part] = lower
        copies.append(
            pltpu.make_async_copy(basis.at[:, part], basis_hbm.at[:, part], basis_sems.at[i])
        )
        copies[-1].start()
    for copy in copies:
        copy.wait()


def shards(latents, test_matrix):
    rows, width = latents.shape
    tall = test_matrix.shape[1]
    row_total = rows * lax.axis_size("blk") * lax.axis_size("inner")
    core = (lax.axis_index("blk") % 2).astype(jnp.int32).reshape(1)
    swap = [(i, i ^ 1) for i in range(2 * CHIPS)]
    groups = [[2 * i + side for i in range(CHIPS)] for side in range(2)]

    def over_chips(value):
        return lax.all_to_all(value, "blk", 0, 0, axis_index_groups=groups)

    high, mid, keep, give = front(core, latents, test_matrix.T, row_total)
    chunks = over_chips(keep + lax.ppermute(give, "blk", swap))
    chunk = lax.all_to_all(sum_copies(chunks, DEPTH), "inner", 0, 0)
    half = over_chips(sum_copies(chunk, CHIPS))
    gram_far = lax.ppermute(half[:, tall // 2 :], "blk", swap)
    half, gram_far = lax.optimization_barrier((half, gram_far))
    other = lax.ppermute(half, "blk", swap)
    inverse = call(
        factor_kernel,
        "factor",
        shape(tall, 384),
        [SMEM, VMEM, VMEM],
        VMEM,
        [pltpu.VMEM((9 * LANES, LANES), jnp.float32)],
        flops=12 * 10**9,
    )(core, half, gram_far)
    bf16 = jnp.bfloat16
    basis_t, projection = call(
        functools.partial(finish_kernel, float(width) ** 0.5 / row_total),
        "finish",
        [shape(tall, rows), shape(tall, width)],
        [SMEM, VMEM, VMEM, VMEM, HBM, HBM],
        [HBM, HBM],
        [
            pltpu.VMEM((tall, rows), bf16),
            pltpu.VMEM((tall, rows), bf16),
            pltpu.VMEM((tall, rows), jnp.float32),
            pltpu.VMEM((tall, width), jnp.float32),
            pltpu.SemaphoreType.DMA((2,)),
            pltpu.SemaphoreType.DMA((BLOCKS,)),
            pltpu.SemaphoreType.DMA((4,)),
        ],
        flops=3 * 10**9,
        moved=10**7,
    )(core, inverse, half, other, high, mid)
    return (basis_t.T, projection)


def solution(mesh):
    placed = (P(("blk", "inner"), None), P())
    return jax.shard_map(
        shards,
        mesh=mesh,
        in_specs=placed,
        out_specs=(P(("blk", "inner"), None), P()),
        check_vma=False,
    )
```

```python
import functools

import jax
import jax.numpy as jnp
from jax import lax
from jax.experimental import pallas as pl
from jax.experimental.pallas import tpu as pltpu
from jax.sharding import PartitionSpec as P

HIGHEST = lax.Precision.HIGHEST
LANES = 128
STEP = 8


def dot(a, b):
    return jnp.dot(a, b, precision=HIGHEST, preferred_element_type=jnp.float32)


def dot_t(a, b):
    return lax.dot_general(
        a, b, (((0,), (0,)), ((), ())), precision=HIGHEST, preferred_element_type=jnp.float32
    )


def factor_inverse(w, n, scratch):
    count = n // 8
    tiles = [w[8 * t : 8 * t + 8, :] for t in range(count)]
    lane = lax.broadcasted_iota(jnp.int32, (8, LANES), 1)
    sub = lax.broadcasted_iota(jnp.int32, (8, LANES), 0)
    pivots = []

    def over_lanes(x, j):
        return jnp.broadcast_to(x[:, j : j + 1], (8, LANES))

    for first in range(count):
        j = STEP * first
        base = 9 * STEP * first
        group = (lane >= j) & (lane < j + STEP)

        def row(i, base=base):
            return jnp.broadcast_to(scratch[base + i : base + i + 1, :], (8, LANES))

        for k in range(STEP):
            scratch[base + 8 * k : base + 8 * k + 8, :] = over_lanes(tiles[first], j + k)
        scratch[base + 64 : base + 72, :] = jnp.where(group, 0.0, tiles[first])
        square = [[row(8 * k + m) for k in range(m + 1)] for m in range(STEP)]
        rows = [row(64 + m) for m in range(STEP)]
        lower = [[None] * STEP for _ in range(STEP)]
        inverse = []
        pivot = square[0][0]
        for k in range(STEP):
            if k:
                pivot = jnp.where(sub == k, square[k][k], pivot)
            inverse.append(1.0 / square[k][k])
            for m in range(k + 1, STEP):
                lower[m][k] = square[m][k] * inverse[k]
            for m in range(k + 1, STEP):
                for i in range(m, STEP):
                    square[i][m] = square[i][m] - square[i][k] * lower[m][k]
            rows[k] = jnp.where(lane == j + k, 1.0, rows[k])
            for m in range(k + 1, STEP):
                rows[m] = rows[m] - lower[m][k] * rows[k]
        pivots.append(pivot)
        done = rows[0]
        for k in range(1, STEP):
            done = jnp.where(sub == k, rows[k], done)
        tiles[first] = done
        scaled = [rows[k] * inverse[k] for k in range(STEP)]
        for t in range(first + 1, count):
            cols = [over_lanes(tiles[t], j + k) for k in range(STEP)]
            x = jnp.where(group, 0.0, tiles[t])
            for k in range(STEP):
                x = x - cols[k] * scaled[k]
                for m in range(k + 1, STEP):
                    cols[m] = cols[m] - cols[k] * lower[m][k]
            tiles[t] = x
    out = []
    for t in range(count):
        out.append(jnp.where(lane <= sub + 8 * t, tiles[t] * lax.rsqrt(pivots[t]), 0.0))
    return jnp.concatenate(out, axis=0)


def bf16_parts(x):
    high = x.astype(jnp.bfloat16)
    return high, (x - high.astype(jnp.float32)).astype(jnp.bfloat16)


def mxu(a, b, dims=((1,), (0,))):
    return lax.dot_general(a, b, (dims, ((), ())), preferred_element_type=jnp.float32)


ROWS_OF = ((1,), (1,))
VMEM = pl.BlockSpec(memory_space=pltpu.VMEM)
SMEM = pl.BlockSpec(memory_space=pltpu.SMEM)
HBM = pl.BlockSpec(memory_space=pltpu.HBM)
CHIPS = 16
DEPTH = 8
LOADS = 3


def shape(*dims, dtype=jnp.float32):
    return jax.ShapeDtypeStruct(dims, dtype)


def call(kernel, name, out_shape, in_specs, out_specs, scratch=(), flops=10**6, moved=10**6, mib=24):
    return pl.pallas_call(
        kernel,
        out_shape=out_shape,
        in_specs=in_specs,
        out_specs=out_specs,
        scratch_shapes=list(scratch),
        compiler_params=pltpu.CompilerParams(vmem_limit_bytes=mib * 2**20),
        cost_estimate=pl.CostEstimate(flops=flops, bytes_accessed=moved, transcendentals=0),
        name=name,
    )


def put_tiles(ref, first, out):
    edge = out.shape[0] // 2
    for j in range(out.shape[1] // LANES * 2):
        rows_from, lanes_from = (j % 2) * edge, (j // 2) * LANES
        ref[first + j, 0:edge, :] = out[
            rows_from : rows_from + edge, lanes_from : lanes_from + LANES
        ]


def front_kernel(
    row_total, core_ref, lat_hbm, om_hbm, high_ref, mid_ref, own_ref, give_ref, lat, om, parts, sems
):
    rows, width = lat.shape
    tall = om.shape[0]
    block = rows // LOADS
    core = core_ref[0]

    def load(i):
        part = pl.ds(i * block, block)
        return pltpu.make_async_copy(lat_hbm.at[part], lat.at[part], sems.at[i])

    test = pltpu.make_async_copy(om_hbm, om, sems.at[LOADS])
    test.start()
    for i in range(LOADS):
        load(i).start()
    test.wait()
    for i in range(LOADS):
        load(i).wait()
        part = pl.ds(i * block, block)
        s = mxu(om[...], lat[part, :], ROWS_OF)
        high, mid = bf16_parts(s)
        low = (s - high.astype(jnp.float32) - mid.astype(jnp.float32)).astype(jnp.bfloat16)
        high_ref[:, part] = high
        mid_ref[:, part] = mid
        parts[0:tall, part] = high
        parts[tall : 2 * tall, part] = mid
        parts[2 * tall :, part] = low

    at = pl.multiple_of((1 - core) * (width // 2), width // 2)
    put_tiles(give_ref, 0, mxu(parts[0:tall, :], lat[:, pl.ds(at, width // 2)]))

    by_high = mxu(parts[0:tall, :], parts[...], ROWS_OF)
    mixed = by_high[:, tall : 2 * tall] + by_high[:, 2 * tall :]
    mid = parts[tall : 2 * tall, :]
    gram = by_high[:, 0:tall] + (mixed + mixed.T + mxu(mid, mid, ROWS_OF))
    gram = gram * (1.0 / row_total)
    corner = jnp.concatenate([gram[256:320, 256:320], gram[64:128, 64:128]], axis=1)
    zero = jnp.concatenate([gram[0:64, 0:128], corner, gram[0:128, 128:256]], axis=0)
    last = jnp.concatenate([gram[0:128, 256:320], gram[128:256, 256:320]], axis=1)
    one = jnp.concatenate([last, gram[128:256, 128:256]], axis=0)
    own = jnp.where(core == 0, zero, one).reshape(CHIPS, 16, LANES)
    far = jnp.where(core == 0, one, zero).reshape(CHIPS, 16, LANES)
    own_ref[...] = own
    give_ref[:, tall // 2 :, :] = far


def front(core, latents, test_t, row_total):
    rows, width = latents.shape
    tall = test_t.shape[0]
    bf16 = jnp.bfloat16
    return call(
        functools.partial(front_kernel, row_total),
        "front",
        [
            shape(tall, rows, dtype=bf16),
            shape(tall, rows, dtype=bf16),
            shape(CHIPS, 16, LANES),
            shape(CHIPS, tall // 2 + 16, LANES),
        ],
        [SMEM, HBM, HBM],
        [VMEM] * 4,
        [
            pltpu.VMEM((rows, width), bf16),
            pltpu.VMEM((tall, width), bf16),
            pltpu.VMEM((3 * tall, rows), bf16),
            pltpu.SemaphoreType.DMA((LOADS + 1,)),
        ],
        flops=6 * 10**9,
        moved=10**7,
        mib=46,
    )(core, latents, test_t)


def keep_kernel(core_ref, lat_hbm, high_ref, own_ref, keep_ref, lat, sems):
    width = lat.shape[2]
    loads = []
    for i in range(2):
        at = pl.multiple_of(core_ref[0] * (2 * width) + i * width, width)
        loads.append(
            pltpu.make_async_copy(lat_hbm.at[:, pl.ds(at, width)], lat.at[i], sems.at[i])
        )
        loads[i].start()
    keep_ref[:, high_ref.shape[0] // 2 :, :] = own_ref[...]
    for i in range(2):
        loads[i].wait()
        put_tiles(keep_ref, i * CHIPS // 2, mxu(high_ref[...], lat[i]))


def keep_half(core, latents, high, own):
    rows, width = latents.shape
    tall = high.shape[0]
    return call(
        keep_kernel,
        "keep",
        shape(CHIPS, tall // 2 + 16, LANES),
        [SMEM, HBM, VMEM, VMEM],
        VMEM,
        [pltpu.VMEM((2, rows, width // 4), jnp.bfloat16), pltpu.SemaphoreType.DMA((2,))],
        flops=10**9,
        moved=5 * 10**6,
        mib=46,
    )(core, latents, high, own)


def sum_copies_kernel(x_ref, out_ref):
    total = x_ref[0]
    for i in range(1, x_ref.shape[0]):
        total = total + x_ref[i]
    for i in range(out_ref.shape[0]):
        out_ref[i] = total


def sum_copies(x, count):
    return call(sum_copies_kernel, "sum_copies", shape(count, *x.shape[1:]), [VMEM], VMEM)(x)


def back_kernel(
    scale, core_ref, half_ref, other_ref, high_hbm, mid_hbm, basis_hbm, proj_hbm,
    high, low, basis, proj, scratch, in_sems, basis_sems, proj_sems,
):
    core = core_ref[0]
    tall, width = proj.shape
    rows = basis.shape[1]
    edge = tall // 2
    loads = [
        pltpu.make_async_copy(high_hbm, high.at[:, pl.ds(0, rows)], in_sems.at[0]),
        pltpu.make_async_copy(mid_hbm, low.at[:, pl.ds(0, rows)], in_sems.at[1]),
    ]
    for load in loads:
        load.start()
    own = half_ref[:, edge:, :].reshape(256, LANES)
    far = other_ref[:, edge:, :].reshape(256, LANES)
    zero = jnp.where(core == 0, own, far)
    one = jnp.where(core == 0, far, own)
    for side, ref in enumerate((half_ref, other_ref)):
        for j in range(CHIPS):
            here = pl.ds(rows + side * (width // 2) + (j // 2) * LANES, LANES)
            part = pl.ds((j % 2) * edge, edge)
            high[part, here], low[part, here] = bf16_parts(ref[j, 0:edge, :])

    def product(first, m):
        count, depth = m.shape
        m_high, m_low = bf16_parts(m)
        m_both = jnp.concatenate([m_high, m_low], axis=0)
        for c in range((rows + width) // 512):
            part = slice(512 * c, 512 * c + 512)
            x_high, x_low = high[0:depth, part], low[0:depth, part]
            by_high = mxu(m_both, x_high)
            y = by_high[:count] + (mxu(m_high, x_low) + by_high[count:])
            if 512 * c < rows:
                basis[first : first + count, part] = y
            else:
                proj[first : first + count, 512 * c - rows : 512 * c + 512 - rows] = y * scale

    copies = []

    def send(i, first, count):
        part = pl.ds(first, count)
        copies.append(
            pltpu.make_async_copy(basis.at[part], basis_hbm.at[part], basis_sems.at[i])
        )
        for side in range(2):
            here = pl.ds(side * (width // 2), width // 2)
            to = core if side == 0 else 1 - core
            there = pl.ds(pl.multiple_of(to * (width // 2), width // 2), width // 2)
            copies.append(
                pltpu.make_async_copy(
                    proj.at[part, here], proj_hbm.at[part, there], proj_sems.at[i, side]
                )
            )
        for copy in copies[-3:]:
            copy.start()

    left = jnp.concatenate([zero[0:64, 64:128].T, zero[64:128, 64:128]], axis=1)
    g00 = jnp.concatenate([zero[0:64], left], axis=0)
    blank = jnp.zeros((128, 64), jnp.float32)
    g01 = jnp.concatenate([zero[128:256], one[0:128, 0:64], blank], axis=1)
    g12 = jnp.concatenate([one[0:128, 64:128], blank], axis=1)
    g22 = jnp.concatenate([zero[64:128, 0:64], blank[0:64]], axis=1)
    m0 = factor_inverse(g00, 128, scratch)
    for load in loads:
        load.wait()
    a01 = dot(m0, g01)
    s11 = one[128:256] - dot_t(a01[:, 0:128], a01[:, 0:128])
    product(0, m0)
    m1 = factor_inverse(s11, 128, scratch)
    s12 = g12 - dot_t(a01[:, 0:128], a01[:, 128:256])
    s22 = g22 - dot_t(a01[:, 128:256], a01[:, 128:256])[0:64]
    b0 = -dot_t(a01, m0)
    send(0, 0, 128)
    a12 = dot(m1, s12)
    s22 = s22 - dot_t(a12, a12)[0:64]
    b10 = dot(m1, b0[0:128])
    product(128, jnp.concatenate([b10, m1], axis=1))
    m2 = factor_inverse(s22, 64, scratch)
    b20 = b0[128:192] - dot_t(a12, b10)[0:64]
    b21 = -dot_t(a12, m1)[0:64]
    send(1, 128, 128)
    m2 = m2[:, 0:64]
    product(256, jnp.concatenate([dot(m2, b20), dot(m2, b21), m2], axis=1))
    send(2, 256, 64)
    for copy in copies:
        copy.wait()


def shards(latents, test_matrix):
    rows, width = latents.shape
    tall = test_matrix.shape[1]
    row_total = rows * lax.axis_size("blk") * lax.axis_size("inner")
    core = (lax.axis_index("blk") % 2).astype(jnp.int32).reshape(1)
    swap = [(i, i ^ 1) for i in range(2 * CHIPS)]
    groups = [[2 * i + side for i in range(CHIPS)] for side in range(2)]

    def over_chips(value):
        return lax.all_to_all(value, "blk", 0, 0, axis_index_groups=groups)

    high, mid, own, give = front(core, latents, test_matrix.T, row_total)
    given = lax.ppermute(give, "blk", swap)
    chunks = over_chips(keep_half(core, latents, high, own) + given)
    chunk = lax.all_to_all(sum_copies(chunks, DEPTH), "inner", 0, 0)
    half = over_chips(sum_copies(chunk, CHIPS))
    other = lax.ppermute(half, "blk", swap)
    bf16 = jnp.bfloat16
    basis_t, projection = call(
        functools.partial(back_kernel, float(width) ** 0.5 / row_total),
        "back",
        [shape(tall, rows), shape(tall, width)],
        [SMEM, VMEM, VMEM, HBM, HBM],
        [HBM, HBM],
        [
            pltpu.VMEM((tall, rows + width), bf16),
            pltpu.VMEM((tall, rows + width), bf16),
            pltpu.VMEM((tall, rows), jnp.float32),
            pltpu.VMEM((tall, width), jnp.float32),
            pltpu.VMEM((9 * LANES, LANES), jnp.float32),
            pltpu.SemaphoreType.DMA((2,)),
            pltpu.SemaphoreType.DMA((3,)),
            pltpu.SemaphoreType.DMA((3, 2)),
        ],
        flops=3 * 10**9,
        moved=10**7,
    )(core, half, other, high, mid)
    return (basis_t.T, projection)


def solution(mesh):
    placed = (P(("blk", "inner"), None), P())
    return jax.shard_map(
        shards,
        mesh=mesh,
        in_specs=placed,
        out_specs=(P(("blk", "inner"), None), P()),
        check_vma=False,
    )
```

```python
import functools

import jax
import jax.numpy as jnp
from jax import lax
from jax.experimental import pallas as pl
from jax.experimental.pallas import tpu as pltpu
from jax.sharding import PartitionSpec as P

HIGHEST = lax.Precision.HIGHEST
LANES = 128
STEP = 8


def dot(a, b):
    return jnp.dot(a, b, precision=HIGHEST, preferred_element_type=jnp.float32)


def dot_t(a, b):
    return lax.dot_general(
        a, b, (((0,), (0,)), ((), ())), precision=HIGHEST, preferred_element_type=jnp.float32
    )


def factor_inverse(w, n, scratch):
    count = n // 8
    tiles = [w[8 * t : 8 * t + 8, :] for t in range(count)]
    lane = lax.broadcasted_iota(jnp.int32, (8, LANES), 1)
    sub = lax.broadcasted_iota(jnp.int32, (8, LANES), 0)
    pivots = []

    def over_lanes(x, j):
        return jnp.broadcast_to(x[:, j : j + 1], (8, LANES))

    for first in range(count):
        j = STEP * first
        base = 9 * STEP * first
        group = (lane >= j) & (lane < j + STEP)

        def row(i, base=base):
            return jnp.broadcast_to(scratch[base + i : base + i + 1, :], (8, LANES))

        for k in range(STEP):
            scratch[base + 8 * k : base + 8 * k + 8, :] = over_lanes(tiles[first], j + k)
        scratch[base + 64 : base + 72, :] = jnp.where(group, 0.0, tiles[first])
        square = [[row(8 * k + m) for k in range(m + 1)] for m in range(STEP)]
        rows = [row(64 + m) for m in range(STEP)]
        lower = [[None] * STEP for _ in range(STEP)]
        inverse = []
        pivot = square[0][0]
        for k in range(STEP):
            if k:
                pivot = jnp.where(sub == k, square[k][k], pivot)
            inverse.append(1.0 / square[k][k])
            for m in range(k + 1, STEP):
                lower[m][k] = square[m][k] * inverse[k]
            for m in range(k + 1, STEP):
                for i in range(m, STEP):
                    square[i][m] = square[i][m] - square[i][k] * lower[m][k]
            rows[k] = jnp.where(lane == j + k, 1.0, rows[k])
            for m in range(k + 1, STEP):
                rows[m] = rows[m] - lower[m][k] * rows[k]
        pivots.append(pivot)
        done = rows[0]
        for k in range(1, STEP):
            done = jnp.where(sub == k, rows[k], done)
        tiles[first] = done
        scaled = [rows[k] * inverse[k] for k in range(STEP)]
        for t in range(first + 1, count):
            cols = [over_lanes(tiles[t], j + k) for k in range(STEP)]
            x = jnp.where(group, 0.0, tiles[t])
            for k in range(STEP):
                x = x - cols[k] * scaled[k]
                for m in range(k + 1, STEP):
                    cols[m] = cols[m] - cols[k] * lower[m][k]
            tiles[t] = x
    out = []
    for t in range(count):
        out.append(jnp.where(lane <= sub + 8 * t, tiles[t] * lax.rsqrt(pivots[t]), 0.0))
    return jnp.concatenate(out, axis=0)


def bf16_parts(x):
    high = x.astype(jnp.bfloat16)
    return high, (x - high.astype(jnp.float32)).astype(jnp.bfloat16)


def mxu(a, b, dims=((1,), (0,))):
    return lax.dot_general(a, b, (dims, ((), ())), preferred_element_type=jnp.float32)


ROWS_OF = ((1,), (1,))
VMEM = pl.BlockSpec(memory_space=pltpu.VMEM)
SMEM = pl.BlockSpec(memory_space=pltpu.SMEM)
HBM = pl.BlockSpec(memory_space=pltpu.HBM)
CHIPS = 16
DEPTH = 8
LOADS = 3


def shape(*dims, dtype=jnp.float32):
    return jax.ShapeDtypeStruct(dims, dtype)


def call(kernel, name, out_shape, in_specs, out_specs, scratch=(), flops=10**6, moved=10**6, mib=24):
    return pl.pallas_call(
        kernel,
        out_shape=out_shape,
        in_specs=in_specs,
        out_specs=out_specs,
        scratch_shapes=list(scratch),
        compiler_params=pltpu.CompilerParams(vmem_limit_bytes=mib * 2**20),
        cost_estimate=pl.CostEstimate(flops=flops, bytes_accessed=moved, transcendentals=0),
        name=name,
    )


def put_tiles(ref, first, out):
    edge = out.shape[0] // 2
    for j in range(out.shape[1] // LANES * 2):
        rows_from, lanes_from = (j % 2) * edge, (j // 2) * LANES
        ref[first + j, 0:edge, :] = out[
            rows_from : rows_from + edge, lanes_from : lanes_from + LANES
        ]


def front_kernel(
    row_total, core_ref, lat_hbm, om_hbm, high_ref, mid_ref, own_ref, give_ref, lat, om, parts, sems
):
    rows, width = lat.shape
    tall = om.shape[0]
    block = rows // LOADS
    core = core_ref[0]

    def load(i):
        part = pl.ds(i * block, block)
        return pltpu.make_async_copy(lat_hbm.at[part], lat.at[part], sems.at[i])

    test = pltpu.make_async_copy(om_hbm, om, sems.at[LOADS])
    test.start()
    for i in range(LOADS):
        load(i).start()
    test.wait()
    for i in range(LOADS):
        load(i).wait()
        part = pl.ds(i * block, block)
        s = mxu(om[...], lat[part, :], ROWS_OF)
        high, mid = bf16_parts(s)
        low = (s - high.astype(jnp.float32) - mid.astype(jnp.float32)).astype(jnp.bfloat16)
        high_ref[:, part] = high
        mid_ref[:, part] = mid
        parts[0:tall, part] = high
        parts[tall : 2 * tall, part] = mid
        parts[2 * tall :, part] = low

    at = pl.multiple_of((1 - core) * (width // 2), width // 2)
    put_tiles(give_ref, 0, mxu(parts[0:tall, :], lat[:, pl.ds(at, width // 2)]))

    by_high = mxu(parts[0:tall, :], parts[...], ROWS_OF)
    mixed = by_high[:, tall : 2 * tall] + by_high[:, 2 * tall :]
    mid = parts[tall : 2 * tall, :]
    gram = by_high[:, 0:tall] + (mixed + mixed.T + mxu(mid, mid, ROWS_OF))
    gram = gram * (1.0 / row_total)
    corner = jnp.concatenate([gram[256:320, 256:320], gram[64:128, 64:128]], axis=1)
    both = jnp.concatenate([gram[0:64, 0:128], corner], axis=0).reshape(CHIPS, 8, LANES)
    last = jnp.concatenate([gram[0:128, 256:320], gram[128:256, 256:320]], axis=1)
    zero = jnp.concatenate([gram[0:128, 128:256], last], axis=0).reshape(CHIPS, 16, LANES)
    one = jnp.concatenate([gram[128:256, 128:256]] * 2, axis=0).reshape(CHIPS, 16, LANES)
    own_ref[:, 0:8, :] = both
    own_ref[:, 8:24, :] = jnp.where(core == 0, zero, one)
    give_ref[:, tall // 2 : tall // 2 + 8, :] = both
    give_ref[:, tall // 2 + 8 :, :] = jnp.where(core == 0, one, zero)


def front(core, latents, test_t, row_total):
    rows, width = latents.shape
    tall = test_t.shape[0]
    bf16 = jnp.bfloat16
    return call(
        functools.partial(front_kernel, row_total),
        "front",
        [
            shape(tall, rows, dtype=bf16),
            shape(tall, rows, dtype=bf16),
            shape(CHIPS, 24, LANES),
            shape(CHIPS, tall // 2 + 24, LANES),
        ],
        [SMEM, HBM, HBM],
        [VMEM] * 4,
        [
            pltpu.VMEM((rows, width), bf16),
            pltpu.VMEM((tall, width), bf16),
            pltpu.VMEM((3 * tall, rows), bf16),
            pltpu.SemaphoreType.DMA((LOADS + 1,)),
        ],
        flops=6 * 10**9,
        moved=10**7,
        mib=46,
    )(core, latents, test_t)


def keep_kernel(core_ref, lat_hbm, high_ref, own_ref, keep_ref, lat, sems):
    width = lat.shape[2]
    loads = []
    for i in range(2):
        at = pl.multiple_of(core_ref[0] * (2 * width) + i * width, width)
        loads.append(
            pltpu.make_async_copy(lat_hbm.at[:, pl.ds(at, width)], lat.at[i], sems.at[i])
        )
        loads[i].start()
    keep_ref[:, high_ref.shape[0] // 2 :, :] = own_ref[...]
    for i in range(2):
        loads[i].wait()
        put_tiles(keep_ref, i * CHIPS // 2, mxu(high_ref[...], lat[i]))


def keep_half(core, latents, high, own):
    rows, width = latents.shape
    tall = high.shape[0]
    return call(
        keep_kernel,
        "keep",
        shape(CHIPS, tall // 2 + 24, LANES),
        [SMEM, HBM, VMEM, VMEM],
        VMEM,
        [pltpu.VMEM((2, rows, width // 4), jnp.bfloat16), pltpu.SemaphoreType.DMA((2,))],
        flops=10**9,
        moved=5 * 10**6,
        mib=46,
    )(core, latents, high, own)


def sum_copies_kernel(x_ref, out_ref):
    total = x_ref[0]
    for i in range(1, x_ref.shape[0]):
        total = total + x_ref[i]
    for i in range(out_ref.shape[0]):
        out_ref[i] = total


def sum_copies(x, count):
    return call(sum_copies_kernel, "sum_copies", shape(count, *x.shape[1:]), [VMEM], VMEM)(x)


def first_kernel(half_ref, high_hbm, mid_hbm, m_ref, high, low, scratch, sems):
    rows = high_hbm.shape[1]
    edge = high.shape[0] // 2
    loads = [
        pltpu.make_async_copy(high_hbm, high.at[:, pl.ds(0, rows)], sems.at[0]),
        pltpu.make_async_copy(mid_hbm, low.at[:, pl.ds(0, rows)], sems.at[1]),
    ]
    for load in loads:
        load.start()
    both = half_ref[:, edge : edge + 8, :].reshape(LANES, LANES)
    left = jnp.concatenate([both[0:64, 64:128].T, both[64:128, 64:128]], axis=1)
    m_ref[...] = factor_inverse(jnp.concatenate([both[0:64], left], axis=0), 128, scratch)
    split_tiles(half_ref, high, low, rows)
    for load in loads:
        load.wait()


def split_tiles(ref, high, low, first):
    edge = high.shape[0] // 2
    for j in range(CHIPS):
        here = pl.ds(first + (j // 2) * LANES, LANES)
        part = pl.ds((j % 2) * edge, edge)
        high[part, here], low[part, here] = bf16_parts(ref[j, 0:edge, :])


def back_kernel(
    scale, core_ref, m_ref, high_ref, low_ref, half_ref, other_ref, basis_hbm, proj_hbm,
    high, low, rest_high, rest_low, basis, proj, scratch, basis_sems, proj_sems,
):
    core = core_ref[0]
    tall, width = proj.shape
    rows = basis.shape[1]
    edge = tall // 2
    own = half_ref[:, edge + 8 :, :].reshape(256, LANES)
    far = other_ref[:, edge + 8 :, :].reshape(256, LANES)
    zero = jnp.where(core == 0, own, far)
    g11 = jnp.where(core == 0, far, own)[0:128]
    split_tiles(other_ref, high, low, 0)

    def columns(c, depth):
        part = slice(512 * c, 512 * c + 512)
        if part.stop <= rows + width // 2:
            return high_ref[depth, part], low_ref[depth, part]
        there = slice(part.start - rows - width // 2, part.stop - rows - width // 2)
        return high[depth, there], low[depth, there]

    def store(first, c, y):
        at = 512 * c
        if at < rows:
            basis[first : first + y.shape[0], at : at + 512] = y
        else:
            proj[first : first + y.shape[0], at - rows : at - rows + 512] = y * scale

    def times(m, x):
        both, m_high = m
        by_high = mxu(both, x[0])
        return by_high[: m_high.shape[0]] + (mxu(m_high, x[1]) + by_high[m_high.shape[0] :])

    def stacked(m):
        m_high, m_low = bf16_parts(m)
        return jnp.concatenate([m_high, m_low], axis=0), m_high

    steps = (rows + width) // 512

    copies = []

    def send(i, first, count):
        part = pl.ds(first, count)
        copies.append(
            pltpu.make_async_copy(basis.at[part], basis_hbm.at[part], basis_sems.at[i])
        )
        for side in range(2):
            here = pl.ds(side * (width // 2), width // 2)
            to = core if side == 0 else 1 - core
            there = pl.ds(pl.multiple_of(to * (width // 2), width // 2), width // 2)
            copies.append(
                pltpu.make_async_copy(
                    proj.at[part, here], proj_hbm.at[part, there], proj_sems.at[i, side]
                )
            )
        for copy in copies[-3:]:
            copy.start()

    blank = jnp.zeros((128, 64), jnp.float32)
    g01 = jnp.concatenate([zero[0:128], zero[128:256, 0:64], blank], axis=1)
    g12 = jnp.concatenate([zero[128:256, 64:128], blank], axis=1)
    corner = half_ref[CHIPS // 2 :, edge : edge + 8, :].reshape(64, LANES)
    g22 = jnp.concatenate([corner[:, 0:64], blank[0:64]], axis=1)
    m0 = m_ref[...]
    a01 = dot(m0, g01)
    s11 = g11 - dot_t(a01[:, 0:128], a01[:, 0:128])
    left = stacked(m0)
    for c in range(steps):
        store(0, c, times(left, columns(c, slice(0, 128))))
    m1 = factor_inverse(s11, 128, scratch)
    s12 = g12 - dot_t(a01[:, 0:128], a01[:, 128:256])
    s22 = g22 - dot_t(a01[:, 128:256], a01[:, 128:256])[0:64]
    b0 = -dot_t(a01, m0)
    send(0, 0, 128)
    a12 = dot(m1, s12)
    s22 = s22 - dot_t(a12, a12)[0:64]
    b10 = dot(m1, b0[0:128])
    b20 = b0[128:192] - dot_t(a12, b10)[0:64]
    b21 = -dot_t(a12, m1)[0:64]
    top = jnp.concatenate([b10, m1], axis=1)
    left = stacked(jnp.concatenate([top, jnp.concatenate([b20, b21], axis=1)], axis=0))
    for c in range(steps):
        y = times(left, columns(c, slice(0, 256)))
        store(128, c, y[0:128])
        x_high, x_low = columns(c, slice(256, 320))
        rest = y[128:192] + (x_high.astype(jnp.float32) + x_low.astype(jnp.float32))
        rest_high[:, 512 * c : 512 * c + 512], rest_low[:, 512 * c : 512 * c + 512] = bf16_parts(
            rest
        )
    m2 = factor_inverse(s22, 64, scratch)
    send(1, 128, 128)
    left = stacked(m2[:, 0:64])
    for c in range(steps):
        part = slice(512 * c, 512 * c + 512)
        store(256, c, times(left, (rest_high[:, part], rest_low[:, part])))
    send(2, 256, 64)
    for copy in copies:
        copy.wait()


def shards(latents, test_matrix):
    rows, width = latents.shape
    tall = test_matrix.shape[1]
    row_total = rows * lax.axis_size("blk") * lax.axis_size("inner")
    core = (lax.axis_index("blk") % 2).astype(jnp.int32).reshape(1)
    swap = [(i, i ^ 1) for i in range(2 * CHIPS)]
    groups = [[2 * i + side for i in range(CHIPS)] for side in range(2)]

    def over_chips(value):
        return lax.all_to_all(value, "blk", 0, 0, axis_index_groups=groups)

    high, mid, own, give = front(core, latents, test_matrix.T, row_total)
    given = lax.ppermute(give, "blk", swap)
    chunks = over_chips(keep_half(core, latents, high, own) + given)
    chunk = lax.all_to_all(sum_copies(chunks, DEPTH), "inner", 0, 0)
    half = over_chips(sum_copies(chunk, CHIPS))
    other = lax.ppermute(half, "blk", swap)
    bf16 = jnp.bfloat16
    ready = rows + width // 2
    inverse, high, low = call(
        first_kernel,
        "first",
        [shape(LANES, LANES)] + [shape(tall, ready, dtype=bf16)] * 2,
        [VMEM, HBM, HBM],
        [VMEM] * 3,
        [pltpu.VMEM((9 * LANES, LANES), jnp.float32), pltpu.SemaphoreType.DMA((2,))],
        flops=4 * 10**9,
    )(half, high, mid)
    basis_t, projection = call(
        functools.partial(back_kernel, float(width) ** 0.5 / row_total),
        "back",
        [shape(tall, rows), shape(tall, width)],
        [SMEM] + [VMEM] * 5,
        [HBM, HBM],
        [
            pltpu.VMEM((tall, width // 2), bf16),
            pltpu.VMEM((tall, width // 2), bf16),
            pltpu.VMEM((64, rows + width), bf16),
            pltpu.VMEM((64, rows + width), bf16),
            pltpu.VMEM((tall, rows), jnp.float32),
            pltpu.VMEM((tall, width), jnp.float32),
            pltpu.VMEM((9 * LANES, LANES), jnp.float32),
            pltpu.SemaphoreType.DMA((3,)),
            pltpu.SemaphoreType.DMA((3, 2)),
        ],
        flops=3 * 10**9,
        moved=10**7,
    )(core, inverse, high, low, half, other)
    return (basis_t.T, projection)


def solution(mesh):
    placed = (P(("blk", "inner"), None), P())
    return jax.shard_map(
        shards,
        mesh=mesh,
        in_specs=placed,
        out_specs=(P(("blk", "inner"), None), P()),
        check_vma=False,
    )
```

```python
import functools

import jax
import jax.numpy as jnp
from jax import lax
from jax.experimental import pallas as pl
from jax.experimental.pallas import tpu as pltpu
from jax.sharding import PartitionSpec as P

HIGHEST = lax.Precision.HIGHEST
LANES = 128
STEP = 8


def dot(a, b):
    return jnp.dot(a, b, precision=HIGHEST, preferred_element_type=jnp.float32)


def dot_t(a, b):
    return lax.dot_general(
        a, b, (((0,), (0,)), ((), ())), precision=HIGHEST, preferred_element_type=jnp.float32
    )


def factor_inverse(w, n, scratch):
    count = n // 8
    tiles = [w[8 * t : 8 * t + 8, :] for t in range(count)]
    lane = lax.broadcasted_iota(jnp.int32, (8, LANES), 1)
    sub = lax.broadcasted_iota(jnp.int32, (8, LANES), 0)
    pivots = []

    on_diagonal = [jnp.where(lane == sub + 8 * t, tiles[t], 0.0) for t in range(count)]
    by_lane = lax.rsqrt(jnp.sum(sum(on_diagonal), axis=0, keepdims=True))
    by_lane = jnp.where(lane < n, jnp.broadcast_to(by_lane, (8, LANES)), 1.0)
    for t in range(count):
        by_row = lax.rsqrt(jnp.sum(on_diagonal[t], axis=1, keepdims=True))
        tiles[t] = tiles[t] * by_lane * by_row

    def over_lanes(x, j):
        return jnp.broadcast_to(x[:, j : j + 1], (8, LANES))

    for first in range(count):
        j = STEP * first
        base = 9 * STEP * first
        group = (lane >= j) & (lane < j + STEP)

        def row(i, base=base):
            return jnp.broadcast_to(scratch[base + i : base + i + 1, :], (8, LANES))

        for k in range(STEP):
            scratch[base + 8 * k : base + 8 * k + 8, :] = over_lanes(tiles[first], j + k)
        scratch[base + 64 : base + 72, :] = jnp.where(group, 0.0, tiles[first])
        square = [[row(8 * k + m) for k in range(m + 1)] for m in range(STEP)]
        rows = [row(64 + m) for m in range(STEP)]
        lower = [[None] * STEP for _ in range(STEP)]
        inverse = [None] * STEP
        pivot = square[0][0]
        for k in range(0, STEP, 2):
            a, b, c = square[k][k], square[k + 1][k], square[k + 1][k + 1]
            determinant = a * c - b * b
            inverse[k] = 1.0 / a
            inverse[k + 1] = a * (1.0 / determinant)
            pivot = jnp.where(sub == k, a, pivot)
            pivot = jnp.where(sub == k + 1, determinant * inverse[k], pivot)
            lower[k + 1][k] = b * inverse[k]
            second = [None] * STEP
            for m in range(k + 2, STEP):
                lower[m][k] = square[m][k] * inverse[k]
                second[m] = square[m][k + 1] - square[m][k] * lower[k + 1][k]
                lower[m][k + 1] = second[m] * inverse[k + 1]
            for m in range(k + 2, STEP):
                for i in range(m, STEP):
                    square[i][m] = (
                        square[i][m] - square[i][k] * lower[m][k] - second[i] * lower[m][k + 1]
                    )
            for q in (k, k + 1):
                rows[q] = jnp.where(lane == j + q, 1.0, rows[q])
                for m in range(q + 1, STEP):
                    rows[m] = rows[m] - lower[m][q] * rows[q]
        pivots.append(pivot)
        done = rows[0]
        for k in range(1, STEP):
            done = jnp.where(sub == k, rows[k], done)
        tiles[first] = done
        scaled = [rows[k] * inverse[k] for k in range(STEP)]
        for t in range(first + 1, count):
            cols = [over_lanes(tiles[t], j + k) for k in range(STEP)]
            x = jnp.where(group, 0.0, tiles[t])
            for k in range(STEP):
                x = x - cols[k] * scaled[k]
                for m in range(k + 1, STEP):
                    cols[m] = cols[m] - cols[k] * lower[m][k]
            tiles[t] = x
    out = []
    for t in range(count):
        out.append(jnp.where(lane <= sub + 8 * t, tiles[t] * lax.rsqrt(pivots[t]) * by_lane, 0.0))
    return jnp.concatenate(out, axis=0)


def bf16_parts(x):
    high = x.astype(jnp.bfloat16)
    return high, (x - high.astype(jnp.float32)).astype(jnp.bfloat16)


def mxu(a, b, dims=((1,), (0,))):
    return lax.dot_general(a, b, (dims, ((), ())), preferred_element_type=jnp.float32)


ROWS_OF = ((1,), (1,))
VMEM = pl.BlockSpec(memory_space=pltpu.VMEM)
SMEM = pl.BlockSpec(memory_space=pltpu.SMEM)
HBM = pl.BlockSpec(memory_space=pltpu.HBM)
CHIPS = 16
DEPTH = 8
LOADS = 3


def shape(*dims, dtype=jnp.float32):
    return jax.ShapeDtypeStruct(dims, dtype)


def call(kernel, name, out_shape, in_specs, out_specs, scratch=(), flops=10**6, moved=10**6, mib=24):
    return pl.pallas_call(
        kernel,
        out_shape=out_shape,
        in_specs=in_specs,
        out_specs=out_specs,
        scratch_shapes=list(scratch),
        compiler_params=pltpu.CompilerParams(vmem_limit_bytes=mib * 2**20),
        cost_estimate=pl.CostEstimate(flops=flops, bytes_accessed=moved, transcendentals=0),
        name=name,
    )


def put_tiles(ref, first, out):
    edge = out.shape[0] // 2
    for j in range(out.shape[1] // LANES * 2):
        rows_from, lanes_from = (j % 2) * edge, (j // 2) * LANES
        ref[first + j, 0:edge, :] = out[
            rows_from : rows_from + edge, lanes_from : lanes_from + LANES
        ]


def front_kernel(
    row_total, core_ref, lat_hbm, om_hbm, high_ref, mid_ref, own_ref, give_ref, lat, om, parts, sems
):
    rows, width = lat.shape
    tall = om.shape[0]
    block = rows // LOADS
    core = core_ref[0]

    def load(i):
        part = pl.ds(i * block, block)
        return pltpu.make_async_copy(lat_hbm.at[part], lat.at[part], sems.at[i])

    test = pltpu.make_async_copy(om_hbm, om, sems.at[LOADS])
    test.start()
    for i in range(LOADS):
        load(i).start()
    test.wait()
    for i in range(LOADS):
        load(i).wait()
        part = pl.ds(i * block, block)
        s = mxu(om[...], lat[part, :], ROWS_OF)
        high, mid = bf16_parts(s)
        low = (s - high.astype(jnp.float32) - mid.astype(jnp.float32)).astype(jnp.bfloat16)
        high_ref[:, part] = high
        mid_ref[:, part] = mid
        parts[0:tall, part] = high
        parts[tall : 2 * tall, part] = mid
        parts[2 * tall :, part] = low

    at = pl.multiple_of((1 - core) * (width // 2), width // 2)
    put_tiles(give_ref, 0, mxu(parts[0:tall, :], lat[:, pl.ds(at, width // 2)]))

    by_high = mxu(parts[0:tall, :], parts[...], ROWS_OF)
    mixed = by_high[:, tall : 2 * tall] + by_high[:, 2 * tall :]
    mid = parts[tall : 2 * tall, :]
    gram = by_high[:, 0:tall] + (mixed + mixed.T + mxu(mid, mid, ROWS_OF))
    gram = gram * (1.0 / row_total)
    corner = jnp.concatenate([gram[256:320, 256:320], gram[64:128, 64:128]], axis=1)
    both = jnp.concatenate([gram[0:64, 0:128], corner], axis=0).reshape(CHIPS, 8, LANES)
    last = jnp.concatenate([gram[0:128, 256:320], gram[128:256, 256:320]], axis=1)
    zero = jnp.concatenate([gram[0:128, 128:256], last], axis=0).reshape(CHIPS, 16, LANES)
    one = jnp.concatenate([gram[128:256, 128:256]] * 2, axis=0).reshape(CHIPS, 16, LANES)
    own_ref[:, 0:8, :] = both
    own_ref[:, 8:24, :] = jnp.where(core == 0, zero, one)
    give_ref[:, tall // 2 : tall // 2 + 8, :] = both
    give_ref[:, tall // 2 + 8 :, :] = jnp.where(core == 0, one, zero)


def front(core, latents, test_t, row_total):
    rows, width = latents.shape
    tall = test_t.shape[0]
    bf16 = jnp.bfloat16
    return call(
        functools.partial(front_kernel, row_total),
        "front",
        [
            shape(tall, rows, dtype=bf16),
            shape(tall, rows, dtype=bf16),
            shape(CHIPS, 24, LANES),
            shape(CHIPS, tall // 2 + 24, LANES),
        ],
        [SMEM, HBM, HBM],
        [VMEM] * 4,
        [
            pltpu.VMEM((rows, width), bf16),
            pltpu.VMEM((tall, width), bf16),
            pltpu.VMEM((3 * tall, rows), bf16),
            pltpu.SemaphoreType.DMA((LOADS + 1,)),
        ],
        flops=6 * 10**9,
        moved=10**7,
        mib=46,
    )(core, latents, test_t)


def keep_kernel(core_ref, lat_hbm, high_ref, own_ref, keep_ref, lat, sems):
    width = lat.shape[2]
    loads = []
    for i in range(2):
        at = pl.multiple_of(core_ref[0] * (2 * width) + i * width, width)
        loads.append(
            pltpu.make_async_copy(lat_hbm.at[:, pl.ds(at, width)], lat.at[i], sems.at[i])
        )
        loads[i].start()
    keep_ref[:, high_ref.shape[0] // 2 :, :] = own_ref[...]
    for i in range(2):
        loads[i].wait()
        put_tiles(keep_ref, i * CHIPS // 2, mxu(high_ref[...], lat[i]))


def keep_half(core, latents, high, own):
    rows, width = latents.shape
    tall = high.shape[0]
    return call(
        keep_kernel,
        "keep",
        shape(CHIPS, tall // 2 + 24, LANES),
        [SMEM, HBM, VMEM, VMEM],
        VMEM,
        [pltpu.VMEM((2, rows, width // 4), jnp.bfloat16), pltpu.SemaphoreType.DMA((2,))],
        flops=10**9,
        moved=5 * 10**6,
        mib=46,
    )(core, latents, high, own)


def sum_copies_kernel(x_ref, out_ref):
    total = x_ref[0]
    for i in range(1, x_ref.shape[0]):
        total = total + x_ref[i]
    for i in range(out_ref.shape[0]):
        out_ref[i] = total


def sum_copies(x, count):
    return call(sum_copies_kernel, "sum_copies", shape(count, *x.shape[1:]), [VMEM], VMEM)(x)


def first_kernel(half_ref, high_hbm, mid_hbm, m_ref, high, low, scratch, sems):
    rows = high_hbm.shape[1]
    edge = high.shape[0] // 2
    loads = [
        pltpu.make_async_copy(high_hbm, high.at[:, pl.ds(0, rows)], sems.at[0]),
        pltpu.make_async_copy(mid_hbm, low.at[:, pl.ds(0, rows)], sems.at[1]),
    ]
    for load in loads:
        load.start()
    both = half_ref[:, edge : edge + 8, :].reshape(LANES, LANES)
    left = jnp.concatenate([both[0:64, 64:128].T, both[64:128, 64:128]], axis=1)
    m_ref[...] = factor_inverse(jnp.concatenate([both[0:64], left], axis=0), 128, scratch)
    split_tiles(half_ref, high, low, rows)
    for load in loads:
        load.wait()


def split_tiles(ref, high, low, first):
    edge = high.shape[0] // 2
    for j in range(CHIPS):
        here = pl.ds(first + (j // 2) * LANES, LANES)
        part = pl.ds((j % 2) * edge, edge)
        high[part, here], low[part, here] = bf16_parts(ref[j, 0:edge, :])


def back_kernel(
    scale, core_ref, m_ref, high_ref, low_ref, half_ref, other_ref, basis_hbm, proj_hbm,
    high, low, rest_high, rest_low, basis, proj, scratch, basis_sems, proj_sems,
):
    core = core_ref[0]
    tall, width = proj.shape
    rows = basis.shape[1]
    edge = tall // 2
    own = half_ref[:, edge + 8 :, :].reshape(256, LANES)
    far = other_ref[:, edge + 8 :, :].reshape(256, LANES)
    zero = jnp.where(core == 0, own, far)
    g11 = jnp.where(core == 0, far, own)[0:128]

    def columns(c, depth):
        part = slice(512 * c, 512 * c + 512)
        if part.stop <= rows + width // 2:
            return high_ref[depth, part], low_ref[depth, part]
        there = slice(part.start - rows - width // 2, part.stop - rows - width // 2)
        return high[depth, there], low[depth, there]

    def store(first, c, y):
        at = 512 * c
        if at < rows:
            basis[first : first + y.shape[0], at : at + 512] = y
        else:
            proj[first : first + y.shape[0], at - rows : at - rows + 512] = y * scale

    def times(m, x):
        both, m_high = m
        by_high = mxu(both, x[0])
        return by_high[: m_high.shape[0]] + (mxu(m_high, x[1]) + by_high[m_high.shape[0] :])

    def stacked(m):
        m_high, m_low = bf16_parts(m)
        return jnp.concatenate([m_high, m_low], axis=0), m_high

    steps = (rows + width) // 512

    copies = []

    def send(i, first, count):
        part = pl.ds(first, count)
        copies.append(
            pltpu.make_async_copy(basis.at[part], basis_hbm.at[part], basis_sems.at[i])
        )
        for side in range(2):
            here = pl.ds(side * (width // 2), width // 2)
            to = core if side == 0 else 1 - core
            there = pl.ds(pl.multiple_of(to * (width // 2), width // 2), width // 2)
            copies.append(
                pltpu.make_async_copy(
                    proj.at[part, here], proj_hbm.at[part, there], proj_sems.at[i, side]
                )
            )
        for copy in copies[-3:]:
            copy.start()

    blank = jnp.zeros((128, 64), jnp.float32)
    g01 = jnp.concatenate([zero[0:128], zero[128:256, 0:64], blank], axis=1)
    g12 = jnp.concatenate([zero[128:256, 64:128], blank], axis=1)
    corner = half_ref[CHIPS // 2 :, edge : edge + 8, :].reshape(64, LANES)
    g22 = jnp.concatenate([corner[:, 0:64], blank[0:64]], axis=1)
    m0 = m_ref[...]
    a01 = dot(m0, g01)
    s11 = g11 - dot_t(a01[:, 0:128], a01[:, 0:128])
    split_tiles(other_ref, high, low, 0)
    left = stacked(m0)
    for c in range(steps):
        store(0, c, times(left, columns(c, slice(0, 128))))
    m1 = factor_inverse(s11, 128, scratch)
    s12 = g12 - dot_t(a01[:, 0:128], a01[:, 128:256])
    s22 = g22 - dot_t(a01[:, 128:256], a01[:, 128:256])[0:64]
    b0 = -dot_t(a01, m0)
    send(0, 0, 128)
    a12 = dot(m1, s12)
    s22 = s22 - dot_t(a12, a12)[0:64]
    b10 = dot(m1, b0[0:128])
    b20 = b0[128:192] - dot_t(a12, b10)[0:64]
    b21 = -dot_t(a12, m1)[0:64]
    top = jnp.concatenate([b10, m1], axis=1)
    left = stacked(jnp.concatenate([top, jnp.concatenate([b20, b21], axis=1)], axis=0))
    for c in range(steps):
        y = times(left, columns(c, slice(0, 256)))
        store(128, c, y[0:128])
        x_high, x_low = columns(c, slice(256, 320))
        rest = y[128:192] + (x_high.astype(jnp.float32) + x_low.astype(jnp.float32))
        rest_high[:, 512 * c : 512 * c + 512], rest_low[:, 512 * c : 512 * c + 512] = bf16_parts(
            rest
        )
    m2 = factor_inverse(s22, 64, scratch)
    send(1, 128, 128)
    left = stacked(m2[:, 0:64])
    for c in range(steps):
        part = slice(512 * c, 512 * c + 512)
        store(256, c, times(left, (rest_high[:, part], rest_low[:, part])))
    send(2, 256, 64)
    for copy in copies:
        copy.wait()


def shards(latents, test_matrix):
    rows, width = latents.shape
    tall = test_matrix.shape[1]
    row_total = rows * lax.axis_size("blk") * lax.axis_size("inner")
    core = (lax.axis_index("blk") % 2).astype(jnp.int32).reshape(1)
    swap = [(i, i ^ 1) for i in range(2 * CHIPS)]
    groups = [[2 * i + side for i in range(CHIPS)] for side in range(2)]

    def over_chips(value):
        return lax.all_to_all(value, "blk", 0, 0, axis_index_groups=groups)

    high, mid, own, give = front(core, latents, test_matrix.T, row_total)
    given = lax.ppermute(give, "blk", swap)
    chunks = over_chips(keep_half(core, latents, high, own) + given)
    chunk = lax.all_to_all(sum_copies(chunks, DEPTH), "inner", 0, 0)
    half = over_chips(sum_copies(chunk, CHIPS))
    other = lax.ppermute(half, "blk", swap)
    bf16 = jnp.bfloat16
    ready = rows + width // 2
    inverse, high, low = call(
        first_kernel,
        "first",
        [shape(LANES, LANES)] + [shape(tall, ready, dtype=bf16)] * 2,
        [VMEM, HBM, HBM],
        [VMEM] * 3,
        [pltpu.VMEM((9 * LANES, LANES), jnp.float32), pltpu.SemaphoreType.DMA((2,))],
        flops=4 * 10**9,
    )(half, high, mid)
    basis_t, projection = call(
        functools.partial(back_kernel, float(width) ** 0.5 / row_total),
        "back",
        [shape(tall, rows), shape(tall, width)],
        [SMEM] + [VMEM] * 5,
        [HBM, HBM],
        [
            pltpu.VMEM((tall, width // 2), bf16),
            pltpu.VMEM((tall, width // 2), bf16),
            pltpu.VMEM((64, rows + width), bf16),
            pltpu.VMEM((64, rows + width), bf16),
            pltpu.VMEM((tall, rows), jnp.float32),
            pltpu.VMEM((tall, width), jnp.float32),
            pltpu.VMEM((9 * LANES, LANES), jnp.float32),
            pltpu.SemaphoreType.DMA((3,)),
            pltpu.SemaphoreType.DMA((3, 2)),
        ],
        flops=3 * 10**9,
        moved=10**7,
    )(core, inverse, high, low, half, other)
    return (basis_t.T, projection)


def solution(mesh):
    placed = (P(("blk", "inner"), None), P())
    return jax.shard_map(
        shards,
        mesh=mesh,
        in_specs=placed,
        out_specs=(P(("blk", "inner"), None), P()),
        check_vma=False,
    )
```
